32 devices in a mesh: groups: 2 (over x), row: 16 (over z, y, core).
Axes of the slice: x: 2, y: 2, z: 4, core: 2. Of those that a mesh axis runs over, the one named last changes fastest.
Arguments:
- amplitudes: bfloat16 [256, 16384], P(('groups', 'row')), parts along dimension 0, may hold values from -6 to 6
- integrals: bfloat16 [16384, 2048], P('row', 'groups'), parts along dimension 1, may hold values from -0.09375 to 0.09375
- constant: float32 [128, 2048], P('row', 'groups'), parts along dimension 1, may hold values from -4 to 4
- occ_pairs: int32 [256, 2], P(('groups', 'row')), parts along dimension 0, may hold values from 0 to 239
- batch_pairs: int32 [2048, 2], P('groups'), parts along dimension 0, may hold values from 0 to 1599
- occ_irrep: int32 [480], P('groups'), parts along dimension 0, may hold values from 0 to 7
- vir_irrep: int32 [3200], P('groups'), parts along dimension 0, may hold values from 0 to 7
- occ_energy: float32 [480], P('groups'), parts along dimension 0, may hold values from -1.5 to -0.3
- vir_energy: float32 [3200], P('groups'), parts along dimension 0, may hold values from 0.2 to 1.5
- t2_pattern: int32 [8, 512], P(None, 'groups'), parts along dimension 1, may hold values 0 or 1
- int_pattern: int32 [512, 8], P(('groups', 'row')), parts along dimension 0, may hold values 0 or 1
Outputs:
- new_amplitudes: float32 [128, 2048], P('row', 'groups'), parts along dimension 1
The draws below stay inside these ranges and needn't reach their ends.
There are 2 independent parts, one for each index of `groups`. The reference program is written for one: setup_inputs(seed, part) draws one part's arguments, and reference() takes and returns one part's arrays. A program takes and returns all parts, laid end to end along the dimension named above; each array names one. Nothing has to cross between parts.
All inputs are finite; a program needn't handle non-finite values. No bound on the sum of `int_pattern` on one device may be relied on, other than what follows from the above.
Results may differ from the reference program's by a relative error of at most 0.0003.
Values may be sent and summed in bfloat16 or wider, within the bound.
A program may use at most 64 MiB of HBM per device.

```python
import jax
import jax.numpy as jnp
from jax import lax

NOCC = 240
NVIRT = 1600
IRREPS = 8
BLOCK = 64
VP_DEV = 1024
OPAIRS = 128
VPAIRS = 16384
VBLOCKS = 256
AB = 1024
N_ROW = 16


def set_ends(values, key, low, high):
    longest = values.shape.index(max(values.shape))
    spots = []
    for shift in (0, 1):
        where = [jax.random.randint(jax.random.fold_in(key, axis), (), 0, length) for axis, length in enumerate(values.shape)]
        where[longest] = (where[longest] + shift) % values.shape[longest]
        spots.append(tuple(where))
    return values.at[spots[0]].set(low).at[spots[1]].set(high)


def block_levels(key, shape, pieces, least, high):
    factor_of, own = 1.0, jax.random.fold_in(key, 6)
    for axis_at, shards_of in pieces:
        draws = jnp.exp(jax.random.uniform(jax.random.fold_in(own, axis_at), (shards_of,), jnp.float32, least / len(pieces), high / len(pieces)))
        factor_of = factor_of * jnp.repeat(draws, shape[axis_at] // shards_of).reshape([-1 if axis == axis_at else 1 for axis in range(len(shape))])
    return factor_of


def centred(own_key, shape, scale, bound, shards=(), kind=jnp.bfloat16):
    result = jax.random.normal(own_key, shape, jnp.float32) * scale
    if len(shards) > 0:
        result = block_levels(own_key, shape, shards, -0.22, 0.18) * result
    return jnp.clip(result, min=-bound, max=bound).astype(kind)


def setup_inputs(seed: int = 0, part: int = 0) -> dict:
    splits = jax.random.split(jax.random.key(seed), 12)
    part_splits = jax.random.split(jax.random.fold_in(splits[11], part), 12)
    amplitudes = centred(part_splits[0], (OPAIRS, VPAIRS), 1.0, 6.0, ((0, 16),))
    integrals = centred(part_splits[1], (VPAIRS, AB), (VPAIRS // 4) ** -0.5, 0.09375, ((0, 16),))
    constant = centred(part_splits[2], (OPAIRS, AB), 0.5, 4.0, ((0, 16),), jnp.float32)
    occ_pairs = set_ends(jax.random.randint(part_splits[3], (OPAIRS, 2), 0, NOCC), jax.random.fold_in(part_splits[3], 1), 0, NOCC - 1).astype(jnp.int32)
    batch_pairs = set_ends(jax.random.randint(part_splits[4], (AB, 2), 0, NVIRT), jax.random.fold_in(part_splits[4], 1), 0, NVIRT - 1).astype(jnp.int32)
    occ_irrep = set_ends(jax.random.randint(part_splits[5], (NOCC,), 0, IRREPS), jax.random.fold_in(part_splits[5], 1), 0, IRREPS - 1).astype(jnp.int32)
    vir_irrep = set_ends(jax.random.randint(part_splits[6], (NVIRT,), 0, IRREPS), jax.random.fold_in(part_splits[6], 1), 0, IRREPS - 1).astype(jnp.int32)
    occ_energy = jnp.clip(jax.random.uniform(part_splits[7], (NOCC,), jnp.float32, -1.5, -0.3), -1.5, -0.3)
    vir_energy = jnp.clip(jax.random.uniform(part_splits[8], (NVIRT,), jnp.float32, 0.2, 1.5), 0.2, 1.5)
    t2_pattern = set_ends((jax.random.randint(part_splits[9], (IRREPS, VBLOCKS), 0, 2) < 1).astype(jnp.int32), jax.random.fold_in(part_splits[9], 1), 0, 1)
    int_pattern = set_ends((jax.random.randint(part_splits[10], (VBLOCKS, IRREPS), 0, 2) < 1).astype(jnp.int32), jax.random.fold_in(part_splits[10], 1), 0, 1)
    return dict(amplitudes=amplitudes, integrals=integrals, constant=constant, occ_pairs=occ_pairs, batch_pairs=batch_pairs, occ_irrep=occ_irrep, vir_irrep=vir_irrep, occ_energy=occ_energy, vir_energy=vir_energy, t2_pattern=t2_pattern, int_pattern=int_pattern)


def reference(amplitudes, integrals, constant, occ_pairs, batch_pairs, occ_irrep, vir_irrep, occ_energy, vir_energy, t2_pattern, int_pattern):
    pair_irrep = jnp.bitwise_xor(occ_irrep[occ_pairs[:, 0]], occ_irrep[occ_pairs[:, 1]])
    batch_irrep = jnp.bitwise_xor(vir_irrep[batch_pairs[:, 0]], vir_irrep[batch_pairs[:, 1]])
    row_pattern = t2_pattern[pair_irrep]
    col_pattern = int_pattern[:, batch_irrep]
    blocks_dev = VP_DEV // BLOCK

    def add_block(running, shard):
        first = shard * VP_DEV
        amps = lax.dynamic_slice_in_dim(amplitudes, first, VP_DEV, 1)
        amask = jnp.repeat(lax.dynamic_slice_in_dim(row_pattern, shard * blocks_dev, blocks_dev, 1), BLOCK, axis=1)
        amps = jnp.where(amask != 0, amps, jnp.zeros((), jnp.bfloat16))
        ints = lax.dynamic_slice_in_dim(integrals, first, VP_DEV, 0)
        imask = jnp.repeat(lax.dynamic_slice_in_dim(col_pattern, shard * blocks_dev, blocks_dev, 0), BLOCK, axis=0)
        ints = jnp.where(imask != 0, ints, jnp.zeros((), jnp.bfloat16))
        product = jnp.dot(amps.astype(jnp.float32), ints.astype(jnp.float32), preferred_element_type=jnp.float32, precision=lax.Precision.HIGHEST)
        return running + product, None

    ladder, unused = lax.scan(add_block, jnp.zeros((OPAIRS, AB), jnp.float32), jnp.arange(N_ROW, dtype=jnp.int32))
    occ_sum = occ_energy[occ_pairs[:, 0]] + occ_energy[occ_pairs[:, 1]]
    vir_sum = vir_energy[batch_pairs[:, 0]] + vir_energy[batch_pairs[:, 1]]
    denom = vir_sum[None, :] - occ_sum[:, None]
    return (constant + ladder) / denom
```

```python
import functools

import jax
import jax.numpy as jnp
from jax import lax
from jax.experimental import pallas as pl
from jax.experimental.pallas import tpu as pltpu
from jax.sharding import PartitionSpec as P

IRREPS = 8
BLOCK = 64
LANES = 128
F32 = jnp.float32
BF16 = jnp.bfloat16


def iota(shape, axis):
    return lax.broadcasted_iota(jnp.int32, shape, axis)


def fold(x):
    half = x.shape[1] // 2
    return jnp.concatenate([x[:, :half], x[:, half:]], axis=0)


def kernel(
    n,
    amps_hbm,
    ints_hbm,
    const_ref,
    occ_pairs_ref,
    batch_pairs_ref,
    occ_irrep_ref,
    vir_irrep_ref,
    occ_energy_ref,
    vir_energy_ref,
    t2_ref,
    intp_ref,
    out_ref,
    amps,
    ints,
    pattern,
    outgoing,
    incoming,
    part,
    from_mate,
    wire_out,
    wire_in,
    local_sem,
    send_sem,
    recv_sem,
    mate_sem,
    wire_sem,
):
    me = lax.axis_index("row")
    chips = n // 2
    core = lax.rem(me, 2)
    chip = me // 2
    mate = me + 1 - 2 * core
    rows = amps.shape[0]
    depth = ints.shape[0]
    width = ints.shape[1]

    barrier = pltpu.get_barrier_semaphore()

    def greet(k, carry):
        pl.semaphore_signal(barrier, inc=1, device_id={"row": lax.rem(me + k, n)}, device_id_type=pl.DeviceIdType.MESH)
        return carry

    get_amps = pltpu.make_async_copy(amps_hbm, amps, local_sem.at[0])
    get_ints = pltpu.make_async_copy(ints_hbm, ints, local_sem.at[1])
    get_amps.start()
    lax.fori_loop(1, n, greet, 0)
    get_ints.start()

    nocc = occ_irrep_ref.shape[1]
    places = iota((rows, nocc), 1)
    first = occ_pairs_ref[:, 0:1] == places
    second = occ_pairs_ref[:, 1:2] == places
    irr = occ_irrep_ref[...]
    en = occ_energy_ref[...]
    pair_irrep = jnp.bitwise_xor(
        jnp.sum(jnp.where(first, irr, 0), axis=1, keepdims=True),
        jnp.sum(jnp.where(second, irr, 0), axis=1, keepdims=True),
    )
    occ_sum = jnp.sum(jnp.where(first, en, 0.0), axis=1, keepdims=True) + jnp.sum(
        jnp.where(second, en, 0.0), axis=1, keepdims=True
    )

    kept = jnp.zeros((rows, t2_ref.shape[1]), jnp.int32)
    for label in range(IRREPS):
        kept = jnp.where(pair_irrep == label, t2_ref[label : label + 1, :], kept)
    pattern[...] = jnp.where(kept != 0, 1.0, 0.0)
    blocks = depth // BLOCK
    per_tile = LANES // blocks
    spread = jnp.where(iota((LANES, depth), 0) == iota((LANES, depth), 1) // BLOCK, 1.0, 0.0).astype(BF16)
    get_amps.wait()

    def mask_tile(tile, carry):
        block_rows = pattern[:, pl.ds(pl.multiple_of(tile * LANES, LANES), LANES)]
        turned = [
            block_rows if k == 0 else pltpu.roll(block_rows, LANES - k * blocks, 1) for k in range(per_tile)
        ]
        mask = jnp.dot(jnp.concatenate(turned, axis=0).astype(BF16), spread, preferred_element_type=F32)
        for k in range(per_tile):
            first_col = pl.multiple_of((tile * per_tile + k) * depth, LANES)
            values = amps[:, pl.ds(first_col, depth)].astype(F32)
            values = jnp.where(mask[k * rows : (k + 1) * rows] != 0.0, values, 0.0)
            outgoing[tile * per_tile + k] = fold(values).astype(BF16)
        return carry

    lax.fori_loop(0, n // per_tile, mask_tile, 0)
    incoming[core * chips + chip] = outgoing[me]

    pl.semaphore_wait(barrier, n - 1)

    def amps_copy(target, parity):
        return pltpu.make_async_remote_copy(
            src_ref=outgoing.at[target],
            dst_ref=incoming.at[core * chips + chip],
            send_sem=send_sem.at[parity],
            recv_sem=recv_sem.at[parity],
            device_id={"row": target},
            device_id_type=pl.DeviceIdType.MESH,
        )

    def send_unlike(k, carry):
        amps_copy(2 * lax.rem(chip + k, chips) + 1 - core, 0).start()
        return carry

    def send_like(k, carry):
        amps_copy(2 * lax.rem(chip + k, chips) + core, 1).start()
        return carry

    lax.fori_loop(0, chips, send_unlike, 0)
    lax.fori_loop(1, chips, send_like, 0)

    nvir = vir_irrep_ref.shape[1]
    highs = -(-nvir // LANES)
    high_rows = -(-highs // 8) * 8

    def table(ref):
        full = nvir // LANES
        pieces = [ref[:, i * LANES : (i + 1) * LANES].astype(F32) for i in range(full)]
        if nvir % LANES:
            rest = ref[:, full * LANES : nvir].astype(F32)
            pieces.append(jnp.concatenate([rest, jnp.zeros((1, LANES - nvir % LANES), F32)], axis=1))
        if high_rows > highs:
            pieces.append(jnp.zeros((high_rows - highs, LANES), F32))
        return jnp.concatenate(pieces, axis=0)

    energies = table(vir_energy_ref)
    top = energies.astype(BF16)
    rest = energies - top.astype(F32)
    middle = rest.astype(BF16)
    last = (rest - middle.astype(F32)).astype(BF16)
    tables = jnp.concatenate([table(vir_irrep_ref).astype(BF16), top, middle, last], axis=0)

    def batch_lookup(row):
        index = batch_pairs_ref[row : row + 1, :]
        low = jnp.bitwise_and(index, LANES - 1)
        high = lax.shift_right_logical(index, 7)
        onehot = jnp.where(iota((LANES, width), 0) == low, 1.0, 0.0).astype(BF16)
        found = jnp.dot(tables, onehot, preferred_element_type=F32)
        pick = iota((high_rows, width), 0) == high
        label = jnp.sum(jnp.where(pick, found[:high_rows], 0.0), axis=0, keepdims=True)
        energy = found[high_rows : 2 * high_rows] + found[2 * high_rows : 3 * high_rows] + found[3 * high_rows :]
        return label.astype(jnp.int32), jnp.sum(jnp.where(pick, energy, 0.0), axis=0, keepdims=True)

    label_a, energy_a = batch_lookup(0)
    label_b, energy_b = batch_lookup(1)
    batch_irrep = jnp.bitwise_xor(label_a, label_b)
    denom = (energy_a + energy_b) - occ_sum

    kept = jnp.zeros((blocks, width), jnp.int32)
    for label in range(IRREPS):
        kept = jnp.where(batch_irrep == label, intp_ref[:, label : label + 1], kept)
    kept = jnp.where(kept != 0, 1.0, 0.0)
    get_ints.wait()
    for b in range(blocks):
        keep = jnp.broadcast_to(kept[b : b + 1], (16, width)).astype(BF16)
        for i in range(BLOCK // 16):
            at = b * BLOCK + i * 16
            ints[at : at + 16, :] = ints[at : at + 16, :] * keep

    group = min(chips, 8)
    half = depth // 2

    def multiply(parity):
        def step(g, carry):
            planes = incoming[pl.ds(parity * chips + g * group, group)].astype(F32)
            left = planes[:, :rows].reshape(group * rows, half).astype(BF16)
            right = planes[:, rows:].reshape(group * rows, half).astype(BF16)
            product = jnp.dot(left, ints[:half, :], preferred_element_type=F32) + jnp.dot(
                right, ints[half:, :], preferred_element_type=F32
            )
            part[parity, pl.ds(g * group, group)] = product.reshape(group, rows, width)
            return carry

        lax.fori_loop(0, chips // group, step, 0)

    def wait_planes(sem, count):
        planes = incoming.at[pl.ds(0, count)]
        pltpu.make_async_copy(planes, planes, sem).wait()

    wait_planes(recv_sem.at[0], chips)
    multiply(1 - core)
    to_mate = pltpu.make_async_remote_copy(
        src_ref=part.at[1 - core],
        dst_ref=from_mate,
        send_sem=mate_sem.at[0],
        recv_sem=mate_sem.at[1],
        device_id={"row": mate},
        device_id_type=pl.DeviceIdType.MESH,
    )
    to_mate.start()
    wait_planes(recv_sem.at[1], chips - 1)
    multiply(core)
    to_mate.wait_recv()

    def wire_copy(target):
        return pltpu.make_async_remote_copy(
            src_ref=wire_out.at[target],
            dst_ref=wire_in.at[chip],
            send_sem=wire_sem.at[0],
            recv_sem=wire_sem.at[1],
            device_id={"row": 2 * target + core},
            device_id_type=pl.DeviceIdType.MESH,
        )

    def send_sum(k, carry):
        target = lax.rem(chip + k, chips)
        wire_out[target] = part[core, target] + from_mate[target]
        wire_copy(target).start()
        return carry

    lax.fori_loop(1, chips, send_sum, 0)
    mine = const_ref[...] + part[core, chip] + from_mate[chip]

    arrived = wire_in.at[pl.ds(0, chips - 1)]
    pltpu.make_async_copy(arrived, arrived, wire_sem.at[1]).wait()

    def add(k, total):
        return total + wire_in[lax.rem(chip + k, chips)]

    total = lax.fori_loop(1, chips, add, mine)
    out_ref[...] = total / denom

    wait_planes(send_sem.at[0], chips)
    wait_planes(send_sem.at[1], chips - 1)
    to_mate.wait_send()
    sent = wire_out.at[pl.ds(0, chips - 1)]
    pltpu.make_async_copy(sent, sent, wire_sem.at[0]).wait()


def per_device(
    n,
    amplitudes,
    integrals,
    constant,
    occ_pairs,
    batch_pairs,
    occ_irrep,
    vir_irrep,
    occ_energy,
    vir_energy,
    t2_pattern,
    int_pattern,
):
    rows = amplitudes.shape[0]
    depth, width = integrals.shape
    chips = n // 2
    vmem = pl.BlockSpec(memory_space=pltpu.VMEM)
    hbm = pl.BlockSpec(memory_space=pl.ANY)
    return pl.pallas_call(
        functools.partial(kernel, n),
        out_shape=jax.ShapeDtypeStruct((rows, width), F32),
        in_specs=[hbm, hbm] + [vmem] * 9,
        out_specs=vmem,
        scratch_shapes=[
            pltpu.VMEM((rows, n * depth), BF16),
            pltpu.VMEM((depth, width), BF16),
            pltpu.VMEM((rows, t2_pattern.shape[1]), F32),
            pltpu.VMEM((n, 2 * rows, depth // 2), BF16),
            pltpu.VMEM((n, 2 * rows, depth // 2), BF16),
            pltpu.VMEM((2, chips, rows, width), F32),
            pltpu.VMEM((chips, rows, width), F32),
            pltpu.VMEM((chips, rows, width), F32),
            pltpu.VMEM((chips, rows, width), F32),
            pltpu.SemaphoreType.DMA((2,)),
            pltpu.SemaphoreType.DMA((2,)),
            pltpu.SemaphoreType.DMA((2,)),
            pltpu.SemaphoreType.DMA((2,)),
            pltpu.SemaphoreType.DMA((2,)),
        ],
        compiler_params=pltpu.CompilerParams(
            collective_id=0, has_side_effects=True, vmem_limit_bytes=60 * 1024 * 1024
        ),
        cost_estimate=pl.CostEstimate(
            flops=2 * n * rows * depth * width, bytes_accessed=2 * depth * width, transcendentals=0
        ),
    )(
        amplitudes,
        integrals,
        constant,
        occ_pairs,
        batch_pairs.T,
        occ_irrep[None, :],
        vir_irrep[None, :],
        occ_energy[None, :],
        vir_energy[None, :],
        t2_pattern,
        int_pattern,
    )


def solution(mesh):
    in_specs = (
        P(("groups", "row"), None),
        P("row", "groups"),
        P("row", "groups"),
        P(("groups", "row"), None),
        P("groups", None),
        P("groups"),
        P("groups"),
        P("groups"),
        P("groups"),
        P(None, "groups"),
        P(("groups", "row"), None),
    )
    out_specs = P("row", "groups")
    return jax.shard_map(
        functools.partial(per_device, mesh.shape["row"]),
        mesh=mesh,
        in_specs=in_specs,
        out_specs=out_specs,
        check_vma=False,
    )
```

```python
import functools

import jax
import jax.numpy as jnp
from jax import lax
from jax.experimental import pallas as pl
from jax.experimental.pallas import tpu as pltpu
from jax.sharding import PartitionSpec as P

IRREPS = 8
BLOCK = 64
LANES = 128
F32 = jnp.float32
BF16 = jnp.bfloat16


def iota(shape, axis):
    return lax.broadcasted_iota(jnp.int32, shape, axis)


def fold(x):
    half = x.shape[1] // 2
    return jnp.concatenate([x[:, :half], x[:, half:]], axis=0)


def upright(row):
    k = row.shape[1]
    square = jnp.broadcast_to(row, (k, k))
    return jnp.sum(jnp.where(iota((k, k), 0) == iota((k, k), 1), square, jnp.zeros_like(square)), axis=1, keepdims=True)


def kernel(
    n,
    amps_hbm,
    ints_hbm,
    const_ref,
    occ_pairs_ref,
    batch_pairs_ref,
    occ_irrep_ref,
    vir_irrep_ref,
    occ_energy_ref,
    vir_energy_ref,
    t2_ref,
    intp_ref,
    out_ref,
    amps,
    ints,
    pattern,
    outgoing,
    incoming,
    part,
    from_mate,
    wire_out,
    wire_in,
    local_sem,
    send_sem,
    recv_sem,
    mate_sem,
    wire_sem,
):
    me = lax.axis_index("row")
    chips = n // 2
    core = lax.rem(me, 2)
    chip = me // 2
    mate = me + 1 - 2 * core
    rows = amps.shape[0]
    depth = ints.shape[0]
    width = ints.shape[1]

    barrier = pltpu.get_barrier_semaphore()

    def greet(k, carry):
        pl.semaphore_signal(barrier, inc=1, device_id={"row": lax.rem(me + k, n)}, device_id_type=pl.DeviceIdType.MESH)
        return carry

    get_amps = pltpu.make_async_copy(amps_hbm, amps, local_sem.at[0])
    get_ints = pltpu.make_async_copy(ints_hbm, ints, local_sem.at[1])
    get_amps.start()
    lax.fori_loop(1, n, greet, 0)
    get_ints.start()

    nocc = occ_irrep_ref.shape[0]
    places = iota((rows, nocc), 1)
    first = upright(occ_pairs_ref[0:1, :]) == places
    second = upright(occ_pairs_ref[1:2, :]) == places
    irr = occ_irrep_ref[...].reshape(1, nocc)
    en = occ_energy_ref[...].reshape(1, nocc)
    pair_irrep = jnp.bitwise_xor(
        jnp.sum(jnp.where(first, irr, 0), axis=1, keepdims=True),
        jnp.sum(jnp.where(second, irr, 0), axis=1, keepdims=True),
    )
    occ_sum = jnp.sum(jnp.where(first, en, 0.0), axis=1, keepdims=True) + jnp.sum(
        jnp.where(second, en, 0.0), axis=1, keepdims=True
    )

    kept = jnp.zeros((rows, t2_ref.shape[1]), jnp.int32)
    for label in range(IRREPS):
        kept = jnp.where(pair_irrep == label, t2_ref[label : label + 1, :], kept)
    pattern[...] = jnp.where(kept != 0, 1.0, 0.0)
    blocks = depth // BLOCK
    per_tile = LANES // blocks
    spread = jnp.where(iota((LANES, depth), 0) == iota((LANES, depth), 1) // BLOCK, 1.0, 0.0).astype(BF16)
    get_amps.wait()

    def mask_tile(tile, carry):
        block_rows = pattern[:, pl.ds(pl.multiple_of(tile * LANES, LANES), LANES)]
        turned = [
            block_rows if k == 0 else pltpu.roll(block_rows, LANES - k * blocks, 1) for k in range(per_tile)
        ]
        mask = jnp.dot(jnp.concatenate(turned, axis=0).astype(BF16), spread, preferred_element_type=F32)
        for k in range(per_tile):
            first_col = pl.multiple_of((tile * per_tile + k) * depth, LANES)
            values = amps[:, pl.ds(first_col, depth)].astype(F32)
            values = jnp.where(mask[k * rows : (k + 1) * rows] != 0.0, values, 0.0)
            outgoing[tile * per_tile + k] = fold(values).astype(BF16)
        return carry

    lax.fori_loop(0, n // per_tile, mask_tile, 0)
    incoming[core * chips + chip] = outgoing[me]

    pl.semaphore_wait(barrier, n - 1)

    def amps_copy(target, parity):
        return pltpu.make_async_remote_copy(
            src_ref=outgoing.at[target],
            dst_ref=incoming.at[core * chips + chip],
            send_sem=send_sem.at[parity],
            recv_sem=recv_sem.at[parity],
            device_id={"row": target},
            device_id_type=pl.DeviceIdType.MESH,
        )

    def send_unlike(k, carry):
        amps_copy(2 * lax.rem(chip + k, chips) + 1 - core, 0).start()
        return carry

    def send_like(k, carry):
        amps_copy(2 * lax.rem(chip + k, chips) + core, 1).start()
        return carry

    lax.fori_loop(0, chips, send_unlike, 0)
    lax.fori_loop(1, chips, send_like, 0)

    nvir = vir_irrep_ref.shape[0]
    highs = -(-nvir // LANES)
    high_rows = -(-highs // 8) * 8

    def table(ref):
        full = nvir // LANES
        pieces = [ref[i * LANES : (i + 1) * LANES].reshape(1, LANES).astype(F32) for i in range(full)]
        if nvir % LANES:
            rest = ref[full * LANES : nvir].reshape(1, nvir - full * LANES).astype(F32)
            pieces.append(jnp.concatenate([rest, jnp.zeros((1, LANES - nvir % LANES), F32)], axis=1))
        if high_rows > highs:
            pieces.append(jnp.zeros((high_rows - highs, LANES), F32))
        return jnp.concatenate(pieces, axis=0)

    energies = table(vir_energy_ref)
    top = energies.astype(BF16)
    rest = energies - top.astype(F32)
    middle = rest.astype(BF16)
    last = (rest - middle.astype(F32)).astype(BF16)
    tables = jnp.concatenate([table(vir_irrep_ref).astype(BF16), top, middle, last], axis=0)

    def batch_lookup(row):
        index = batch_pairs_ref[row : row + 1, :]
        low = jnp.bitwise_and(index, LANES - 1)
        high = lax.shift_right_logical(index, 7)
        onehot = jnp.where(iota((LANES, width), 0) == low, 1.0, 0.0).astype(BF16)
        found = jnp.dot(tables, onehot, preferred_element_type=F32)
        pick = iota((high_rows, width), 0) == high
        label = jnp.sum(jnp.where(pick, found[:high_rows], 0.0), axis=0, keepdims=True)
        energy = found[high_rows : 2 * high_rows] + found[2 * high_rows : 3 * high_rows] + found[3 * high_rows :]
        return label.astype(jnp.int32), jnp.sum(jnp.where(pick, energy, 0.0), axis=0, keepdims=True)

    label_a, energy_a = batch_lookup(0)
    label_b, energy_b = batch_lookup(1)
    batch_irrep = jnp.bitwise_xor(label_a, label_b)
    denom = (energy_a + energy_b) - occ_sum

    kept = jnp.zeros((blocks, width), jnp.int32)
    for label in range(IRREPS):
        kept = jnp.where(batch_irrep == label, upright(intp_ref[label : label + 1, :]), kept)
    kept = jnp.where(kept != 0, 1.0, 0.0)
    get_ints.wait()
    for b in range(blocks):
        keep = jnp.broadcast_to(kept[b : b + 1], (16, width)).astype(BF16)
        for i in range(BLOCK // 16):
            at = b * BLOCK + i * 16
            ints[at : at + 16, :] = ints[at : at + 16, :] * keep

    group = min(chips, 8)
    half = depth // 2

    def multiply(parity):
        def step(g, carry):
            planes = incoming[pl.ds(parity * chips + g * group, group)].astype(F32)
            left = planes[:, :rows].reshape(group * rows, half).astype(BF16)
            right = planes[:, rows:].reshape(group * rows, half).astype(BF16)
            product = jnp.dot(left, ints[:half, :], preferred_element_type=F32) + jnp.dot(
                right, ints[half:, :], preferred_element_type=F32
            )
            part[parity, pl.ds(g * group, group)] = product.reshape(group, rows, width)
            return carry

        lax.fori_loop(0, chips // group, step, 0)

    def wait_planes(sem, count):
        planes = incoming.at[pl.ds(0, count)]
        pltpu.make_async_copy(planes, planes, sem).wait()

    wait_planes(recv_sem.at[0], chips)
    multiply(1 - core)
    to_mate = pltpu.make_async_remote_copy(
        src_ref=part.at[1 - core],
        dst_ref=from_mate,
        send_sem=mate_sem.at[0],
        recv_sem=mate_sem.at[1],
        device_id={"row": mate},
        device_id_type=pl.DeviceIdType.MESH,
    )
    to_mate.start()
    wait_planes(recv_sem.at[1], chips - 1)
    multiply(core)
    to_mate.wait_recv()

    def wire_copy(target):
        return pltpu.make_async_remote_copy(
            src_ref=wire_out.at[target],
            dst_ref=wire_in.at[chip],
            send_sem=wire_sem.at[0],
            recv_sem=wire_sem.at[1],
            device_id={"row": 2 * target + core},
            device_id_type=pl.DeviceIdType.MESH,
        )

    def send_sum(k, carry):
        target = lax.rem(chip + k, chips)
        wire_out[target] = part[core, target] + from_mate[target]
        wire_copy(target).start()
        return carry

    lax.fori_loop(1, chips, send_sum, 0)
    mine = const_ref[...] + part[core, chip] + from_mate[chip]

    arrived = wire_in.at[pl.ds(0, chips - 1)]
    pltpu.make_async_copy(arrived, arrived, wire_sem.at[1]).wait()

    def add(k, total):
        return total + wire_in[lax.rem(chip + k, chips)]

    total = lax.fori_loop(1, chips, add, mine)
    out_ref[...] = total / denom

    wait_planes(send_sem.at[0], chips)
    wait_planes(send_sem.at[1], chips - 1)
    to_mate.wait_send()
    sent = wire_out.at[pl.ds(0, chips - 1)]
    pltpu.make_async_copy(sent, sent, wire_sem.at[0]).wait()


def per_device(
    n,
    amplitudes,
    integrals,
    constant,
    occ_pairs,
    batch_pairs,
    occ_irrep,
    vir_irrep,
    occ_energy,
    vir_energy,
    t2_pattern,
    int_pattern,
):
    rows = amplitudes.shape[0]
    depth, width = integrals.shape
    chips = n // 2
    vmem = pl.BlockSpec(memory_space=pltpu.VMEM)
    hbm = pl.BlockSpec(memory_space=pl.ANY)
    return pl.pallas_call(
        functools.partial(kernel, n),
        out_shape=jax.ShapeDtypeStruct((rows, width), F32),
        in_specs=[hbm, hbm] + [vmem] * 9,
        out_specs=vmem,
        scratch_shapes=[
            pltpu.VMEM((rows, n * depth), BF16),
            pltpu.VMEM((depth, width), BF16),
            pltpu.VMEM((rows, t2_pattern.shape[1]), F32),
            pltpu.VMEM((n, 2 * rows, depth // 2), BF16),
            pltpu.VMEM((n, 2 * rows, depth // 2), BF16),
            pltpu.VMEM((2, chips, rows, width), F32),
            pltpu.VMEM((chips, rows, width), F32),
            pltpu.VMEM((chips, rows, width), F32),
            pltpu.VMEM((chips, rows, width), F32),
            pltpu.SemaphoreType.DMA((2,)),
            pltpu.SemaphoreType.DMA((2,)),
            pltpu.SemaphoreType.DMA((2,)),
            pltpu.SemaphoreType.DMA((2,)),
            pltpu.SemaphoreType.DMA((2,)),
        ],
        compiler_params=pltpu.CompilerParams(
            collective_id=0, has_side_effects=True, vmem_limit_bytes=60 * 1024 * 1024
        ),
        cost_estimate=pl.CostEstimate(
            flops=2 * n * rows * depth * width, bytes_accessed=2 * depth * width, transcendentals=0
        ),
    )(
        amplitudes,
        integrals,
        constant,
        occ_pairs.T,
        batch_pairs.T,
        occ_irrep,
        vir_irrep,
        occ_energy,
        vir_energy,
        t2_pattern,
        int_pattern.T,
    )


def solution(mesh):
    in_specs = (
        P(("groups", "row"), None),
        P("row", "groups"),
        P("row", "groups"),
        P(("groups", "row"), None),
        P("groups", None),
        P("groups"),
        P("groups"),
        P("groups"),
        P("groups"),
        P(None, "groups"),
        P(("groups", "row"), None),
    )
    out_specs = P("row", "groups")
    return jax.shard_map(
        functools.partial(per_device, mesh.shape["row"]),
        mesh=mesh,
        in_specs=in_specs,
        out_specs=out_specs,
        check_vma=False,
    )
```

```python
import functools

import jax
import jax.numpy as jnp
from jax import lax
from jax.experimental import pallas as pl
from jax.experimental.pallas import tpu as pltpu
from jax.sharding import PartitionSpec as P

IRREPS = 8
BLOCK = 64
LANES = 128
F32 = jnp.float32
BF16 = jnp.bfloat16
LEVELS = 32766.0
TINY = 1e-30


def iota(shape, axis):
    return lax.broadcasted_iota(jnp.int32, shape, axis)


def fold(x):
    half = x.shape[1] // 2
    return jnp.concatenate([x[:, :half], x[:, half:]], axis=0)


def unfold(x):
    half = x.shape[0] // 2
    return jnp.concatenate([x[:half], x[half:]], axis=1)


def upright(row):
    k = row.shape[1]
    square = jnp.broadcast_to(row, (k, k))
    return jnp.sum(jnp.where(iota((k, k), 0) == iota((k, k), 1), square, jnp.zeros_like(square)), axis=1, keepdims=True)


def flat(column):
    k = column.shape[0]
    return jnp.sum(jnp.where(iota((k, LANES), 0) == iota((k, LANES), 1), column, 0.0), axis=0, keepdims=True)


def kernel(
    n,
    amps_hbm,
    ints_hbm,
    const_ref,
    occ_pairs_ref,
    batch_pairs_ref,
    occ_irrep_ref,
    vir_irrep_ref,
    occ_energy_ref,
    vir_energy_ref,
    t2_ref,
    intp_ref,
    out_ref,
    amps,
    ints,
    pattern,
    outgoing,
    incoming,
    part,
    from_mate,
    wire_out,
    wire_in,
    step_out,
    step_in,
    local_sem,
    send_sem,
    recv_sem,
    mate_sem,
    wire_sem,
):
    me = lax.axis_index("row")
    chips = n // 2
    core = lax.rem(me, 2)
    chip = me // 2
    mate = me + 1 - 2 * core
    rows = amps.shape[0]
    depth = ints.shape[0]
    width = ints.shape[1]

    barrier = pltpu.get_barrier_semaphore()

    def greet(k, carry):
        pl.semaphore_signal(barrier, inc=1, device_id={"row": lax.rem(me + k, n)}, device_id_type=pl.DeviceIdType.MESH)
        return carry

    get_amps = pltpu.make_async_copy(amps_hbm, amps, local_sem.at[0])
    get_ints = pltpu.make_async_copy(ints_hbm, ints, local_sem.at[1])
    get_amps.start()
    lax.fori_loop(1, n, greet, 0)
    get_ints.start()

    nocc = occ_irrep_ref.shape[0]
    places = iota((rows, nocc), 1)
    first = upright(occ_pairs_ref[0:1, :]) == places
    second = upright(occ_pairs_ref[1:2, :]) == places
    irr = occ_irrep_ref[...].reshape(1, nocc)
    en = occ_energy_ref[...].reshape(1, nocc)
    pair_irrep = jnp.bitwise_xor(
        jnp.sum(jnp.where(first, irr, 0), axis=1, keepdims=True),
        jnp.sum(jnp.where(second, irr, 0), axis=1, keepdims=True),
    )
    occ_sum = jnp.sum(jnp.where(first, en, 0.0), axis=1, keepdims=True) + jnp.sum(
        jnp.where(second, en, 0.0), axis=1, keepdims=True
    )

    kept = jnp.zeros((rows, t2_ref.shape[1]), jnp.int32)
    for label in range(IRREPS):
        kept = jnp.where(pair_irrep == label, t2_ref[label : label + 1, :], kept)
    pattern[...] = jnp.where(kept != 0, 1.0, 0.0)
    blocks = depth // BLOCK
    per_tile = LANES // blocks
    spread = jnp.where(iota((LANES, depth), 0) == iota((LANES, depth), 1) // BLOCK, 1.0, 0.0).astype(BF16)
    get_amps.wait()

    def mask_tile(tile, carry):
        block_rows = pattern[:, pl.ds(pl.multiple_of(tile * LANES, LANES), LANES)]
        turned = [
            block_rows if k == 0 else pltpu.roll(block_rows, LANES - k * blocks, 1) for k in range(per_tile)
        ]
        mask = jnp.dot(jnp.concatenate(turned, axis=0).astype(BF16), spread, preferred_element_type=F32)
        for k in range(per_tile):
            first_col = pl.multiple_of((tile * per_tile + k) * depth, LANES)
            values = amps[:, pl.ds(first_col, depth)].astype(F32)
            values = jnp.where(mask[k * rows : (k + 1) * rows] != 0.0, values, 0.0)
            outgoing[tile * per_tile + k] = fold(values).astype(BF16)
        return carry

    lax.fori_loop(0, n // per_tile, mask_tile, 0)
    incoming[core * chips + chip] = outgoing[me]

    pl.semaphore_wait(barrier, n - 1)

    def amps_copy(target, parity):
        return pltpu.make_async_remote_copy(
            src_ref=outgoing.at[target],
            dst_ref=incoming.at[core * chips + chip],
            send_sem=send_sem.at[parity],
            recv_sem=recv_sem.at[parity],
            device_id={"row": target},
            device_id_type=pl.DeviceIdType.MESH,
        )

    def send_unlike(k, carry):
        amps_copy(2 * lax.rem(chip + k, chips) + 1 - core, 0).start()
        return carry

    def send_like(k, carry):
        amps_copy(2 * lax.rem(chip + k, chips) + core, 1).start()
        return carry

    lax.fori_loop(0, chips, send_unlike, 0)
    lax.fori_loop(1, chips, send_like, 0)

    nvir = vir_irrep_ref.shape[0]
    highs = -(-nvir // LANES)
    high_rows = -(-highs // 8) * 8

    def table(ref):
        full = nvir // LANES
        pieces = [ref[i * LANES : (i + 1) * LANES].reshape(1, LANES).astype(F32) for i in range(full)]
        if nvir % LANES:
            rest = ref[full * LANES : nvir].reshape(1, nvir - full * LANES).astype(F32)
            pieces.append(jnp.concatenate([rest, jnp.zeros((1, LANES - nvir % LANES), F32)], axis=1))
        if high_rows > highs:
            pieces.append(jnp.zeros((high_rows - highs, LANES), F32))
        return jnp.concatenate(pieces, axis=0)

    energies = table(vir_energy_ref)
    top = energies.astype(BF16)
    rest = energies - top.astype(F32)
    middle = rest.astype(BF16)
    last = (rest - middle.astype(F32)).astype(BF16)
    tables = jnp.concatenate([table(vir_irrep_ref).astype(BF16), top, middle, last], axis=0)

    def batch_lookup(row):
        index = batch_pairs_ref[row : row + 1, :]
        low = jnp.bitwise_and(index, LANES - 1)
        high = lax.shift_right_logical(index, 7)
        onehot = jnp.where(iota((LANES, width), 0) == low, 1.0, 0.0).astype(BF16)
        found = jnp.dot(tables, onehot, preferred_element_type=F32)
        pick = iota((high_rows, width), 0) == high
        label = jnp.sum(jnp.where(pick, found[:high_rows], 0.0), axis=0, keepdims=True)
        energy = found[high_rows : 2 * high_rows] + found[2 * high_rows : 3 * high_rows] + found[3 * high_rows :]
        return label.astype(jnp.int32), jnp.sum(jnp.where(pick, energy, 0.0), axis=0, keepdims=True)

    label_a, energy_a = batch_lookup(0)
    label_b, energy_b = batch_lookup(1)
    batch_irrep = jnp.bitwise_xor(label_a, label_b)
    denom = (energy_a + energy_b) - occ_sum

    kept = jnp.zeros((blocks, width), jnp.int32)
    for label in range(IRREPS):
        kept = jnp.where(batch_irrep == label, upright(intp_ref[label : label + 1, :]), kept)
    kept = jnp.where(kept != 0, 1.0, 0.0)
    get_ints.wait()
    for b in range(blocks):
        keep = jnp.broadcast_to(kept[b : b + 1], (16, width)).astype(BF16)
        for i in range(BLOCK // 16):
            at = b * BLOCK + i * 16
            ints[at : at + 16, :] = ints[at : at + 16, :] * keep

    group = min(chips, 8)
    half = depth // 2

    def multiply(parity):
        def step(g, carry):
            planes = incoming[pl.ds(parity * chips + g * group, group)].astype(F32)
            left = planes[:, :rows].reshape(group * rows, half).astype(BF16)
            right = planes[:, rows:].reshape(group * rows, half).astype(BF16)
            product = jnp.dot(left, ints[:half, :], preferred_element_type=F32) + jnp.dot(
                right, ints[half:, :], preferred_element_type=F32
            )
            part[parity, pl.ds(g * group, group)] = product.reshape(group, rows, width)
            return carry

        lax.fori_loop(0, chips // group, step, 0)

    def wait_planes(sem, count):
        planes = incoming.at[pl.ds(0, count)]
        pltpu.make_async_copy(planes, planes, sem).wait()

    wait_planes(recv_sem.at[0], chips)
    multiply(1 - core)
    to_mate = pltpu.make_async_remote_copy(
        src_ref=part.at[1 - core],
        dst_ref=from_mate,
        send_sem=mate_sem.at[0],
        recv_sem=mate_sem.at[1],
        device_id={"row": mate},
        device_id_type=pl.DeviceIdType.MESH,
    )
    to_mate.start()
    wait_planes(recv_sem.at[1], chips - 1)
    multiply(core)
    to_mate.wait_recv()

    def wire_copy(target):
        return pltpu.make_async_remote_copy(
            src_ref=wire_out.at[target],
            dst_ref=wire_in.at[chip],
            send_sem=wire_sem.at[0],
            recv_sem=wire_sem.at[1],
            device_id={"row": 2 * target + core},
            device_id_type=pl.DeviceIdType.MESH,
        )

    def step_copy(target):
        return pltpu.make_async_remote_copy(
            src_ref=step_out.at[target],
            dst_ref=step_in.at[chip],
            send_sem=wire_sem.at[2],
            recv_sem=wire_sem.at[3],
            device_id={"row": 2 * target + core},
            device_id_type=pl.DeviceIdType.MESH,
        )

    def send_sum(k, carry):
        target = lax.rem(chip + k, chips)
        both = part[core, target] + from_mate[target]
        step = jnp.maximum(jnp.max(jnp.abs(both), axis=1, keepdims=True), TINY) * (1.0 / LEVELS)
        step_out[target] = flat(step)
        step_copy(target).start()
        wire_out[target] = fold(jnp.round(both * (1.0 / step))).astype(jnp.int32).astype(jnp.int16)
        wire_copy(target).start()
        return carry

    lax.fori_loop(1, chips, send_sum, 0)
    mine = const_ref[...] + part[core, chip] + from_mate[chip]

    arrived = wire_in.at[pl.ds(0, chips - 1)]
    steps_arrived = step_in.at[pl.ds(0, chips - 1)]
    pltpu.make_async_copy(steps_arrived, steps_arrived, wire_sem.at[3]).wait()
    pltpu.make_async_copy(arrived, arrived, wire_sem.at[1]).wait()

    def add(k, total):
        source = lax.rem(chip + k, chips)
        codes = unfold(wire_in[source].astype(jnp.int32).astype(F32))
        return total + codes * upright(step_in[source][:, :rows])

    total = lax.fori_loop(1, chips, add, mine)
    out_ref[...] = total / denom

    wait_planes(send_sem.at[0], chips)
    wait_planes(send_sem.at[1], chips - 1)
    to_mate.wait_send()
    sent = wire_out.at[pl.ds(0, chips - 1)]
    pltpu.make_async_copy(sent, sent, wire_sem.at[0]).wait()
    steps_sent = step_out.at[pl.ds(0, chips - 1)]
    pltpu.make_async_copy(steps_sent, steps_sent, wire_sem.at[2]).wait()


def per_device(
    n,
    amplitudes,
    integrals,
    constant,
    occ_pairs,
    batch_pairs,
    occ_irrep,
    vir_irrep,
    occ_energy,
    vir_energy,
    t2_pattern,
    int_pattern,
):
    rows = amplitudes.shape[0]
    depth, width = integrals.shape
    chips = n // 2
    vmem = pl.BlockSpec(memory_space=pltpu.VMEM)
    hbm = pl.BlockSpec(memory_space=pl.ANY)
    return pl.pallas_call(
        functools.partial(kernel, n),
        out_shape=jax.ShapeDtypeStruct((rows, width), F32),
        in_specs=[hbm, hbm] + [vmem] * 9,
        out_specs=vmem,
        scratch_shapes=[
            pltpu.VMEM((rows, n * depth), BF16),
            pltpu.VMEM((depth, width), BF16),
            pltpu.VMEM((rows, t2_pattern.shape[1]), F32),
            pltpu.VMEM((n, 2 * rows, depth // 2), BF16),
            pltpu.VMEM((n, 2 * rows, depth // 2), BF16),
            pltpu.VMEM((2, chips, rows, width), F32),
            pltpu.VMEM((chips, rows, width), F32),
            pltpu.VMEM((chips, 2 * rows, width // 2), jnp.int16),
            pltpu.VMEM((chips, 2 * rows, width // 2), jnp.int16),
            pltpu.VMEM((chips, 1, LANES), F32),
            pltpu.VMEM((chips, 1, LANES), F32),
            pltpu.SemaphoreType.DMA((2,)),
            pltpu.SemaphoreType.DMA((2,)),
            pltpu.SemaphoreType.DMA((2,)),
            pltpu.SemaphoreType.DMA((2,)),
            pltpu.SemaphoreType.DMA((4,)),
        ],
        compiler_params=pltpu.CompilerParams(
            collective_id=0, has_side_effects=True, vmem_limit_bytes=60 * 1024 * 1024
        ),
        cost_estimate=pl.CostEstimate(
            flops=2 * n * rows * depth * width, bytes_accessed=2 * depth * width, transcendentals=0
        ),
    )(
        amplitudes,
        integrals,
        constant,
        occ_pairs.T,
        batch_pairs.T,
        occ_irrep,
        vir_irrep,
        occ_energy,
        vir_energy,
        t2_pattern,
        int_pattern.T,
    )


def solution(mesh):
    in_specs = (
        P(("groups", "row"), None),
        P("row", "groups"),
        P("row", "groups"),
        P(("groups", "row"), None),
        P("groups", None),
        P("groups"),
        P("groups"),
        P("groups"),
        P("groups"),
        P(None, "groups"),
        P(("groups", "row"), None),
    )
    out_specs = P("row", "groups")
    return jax.shard_map(
        functools.partial(per_device, mesh.shape["row"]),
        mesh=mesh,
        in_specs=in_specs,
        out_specs=out_specs,
        check_vma=False,
    )
```

```python
import functools

import jax
import jax.numpy as jnp
from jax import lax
from jax.experimental import pallas as pl
from jax.experimental.pallas import tpu as pltpu
from jax.sharding import PartitionSpec as P

IRREPS = 8
BLOCK = 64
LANES = 128
F32 = jnp.float32
BF16 = jnp.bfloat16
LEVELS = 32766.0
TINY = 1e-30


def iota(shape, axis):
    return lax.broadcasted_iota(jnp.int32, shape, axis)


def fold(x):
    half = x.shape[1] // 2
    return jnp.concatenate([x[:, :half], x[:, half:]], axis=0)


def upright(row):
    k = row.shape[1]
    square = jnp.broadcast_to(row, (k, k))
    return jnp.sum(jnp.where(iota((k, k), 0) == iota((k, k), 1), square, jnp.zeros_like(square)), axis=1, keepdims=True)


def flat(column):
    shape = column.shape[1], LANES
    return jnp.sum(jnp.where((iota(shape, 0) == iota(shape, 1))[None], column, 0.0), axis=1, keepdims=True)


def tall(row, k):
    shape = k, LANES
    return jnp.sum(jnp.where((iota(shape, 0) == iota(shape, 1))[None], row, 0.0), axis=2, keepdims=True)


def kernel(
    n,
    amps_hbm,
    ints_hbm,
    const_hbm,
    occ_pairs_hbm,
    batch_pairs_hbm,
    occ_irrep_hbm,
    vir_irrep_hbm,
    occ_energy_hbm,
    vir_energy_hbm,
    t2_hbm,
    intp_hbm,
    out_ref,
    amps,
    ints,
    const_ref,
    occ_pairs_ref,
    batch_pairs_ref,
    occ_irrep_ref,
    vir_irrep_ref,
    occ_energy_ref,
    vir_energy_ref,
    t2_ref,
    intp_ref,
    pattern,
    outgoing,
    incoming,
    part,
    from_mate,
    wire_out,
    wire_in,
    step_out,
    step_in,
    local_sem,
    send_sem,
    recv_sem,
    mate_sem,
    wire_sem,
):
    me = lax.axis_index("row")
    chips = n // 2
    core = lax.rem(me, 2)
    chip = me // 2
    mate = me + 1 - 2 * core
    rows = amps.shape[0]
    depth = ints.shape[0]
    width = ints.shape[1]

    unroll = n <= 16
    barrier = pltpu.get_barrier_semaphore()

    def greet(k, carry):
        pl.semaphore_signal(barrier, inc=1, device_id={"row": lax.rem(me + k, n)}, device_id_type=pl.DeviceIdType.MESH)
        return carry

    get_amps = pltpu.make_async_copy(amps_hbm, amps, local_sem.at[0])
    get_ints = pltpu.make_async_copy(ints_hbm, ints, local_sem.at[1])
    early = [(occ_pairs_hbm, occ_pairs_ref), (occ_irrep_hbm, occ_irrep_ref), (occ_energy_hbm, occ_energy_ref), (t2_hbm, t2_ref)]
    late = [
        (batch_pairs_hbm, batch_pairs_ref),
        (vir_irrep_hbm, vir_irrep_ref),
        (vir_energy_hbm, vir_energy_ref),
        (intp_hbm, intp_ref),
        (const_hbm, const_ref),
    ]
    get_early = [pltpu.make_async_copy(a, b, local_sem.at[2 + i]) for i, (a, b) in enumerate(early)]
    get_late = [pltpu.make_async_copy(a, b, local_sem.at[6 + i]) for i, (a, b) in enumerate(late)]
    for copy in get_early:
        copy.start()
    get_amps.start()
    lax.fori_loop(1, n, greet, 0, unroll=unroll)
    for copy in get_late:
        copy.start()
    get_ints.start()
    for copy in get_early:
        copy.wait()

    nocc = occ_irrep_ref.shape[0]
    places = iota((rows, nocc), 1)
    first = upright(occ_pairs_ref[0:1, :]) == places
    second = upright(occ_pairs_ref[1:2, :]) == places
    irr = occ_irrep_ref[...].reshape(1, nocc)
    en = occ_energy_ref[...].reshape(1, nocc)
    pair_irrep = jnp.bitwise_xor(
        jnp.sum(jnp.where(first, irr, 0), axis=1, keepdims=True),
        jnp.sum(jnp.where(second, irr, 0), axis=1, keepdims=True),
    )
    occ_sum = jnp.sum(jnp.where(first, en, 0.0), axis=1, keepdims=True) + jnp.sum(
        jnp.where(second, en, 0.0), axis=1, keepdims=True
    )

    kept = jnp.zeros((rows, t2_ref.shape[1]), jnp.int32)
    for label in range(IRREPS):
        kept = jnp.where(pair_irrep == label, t2_ref[label : label + 1, :], kept)
    pattern[...] = jnp.where(kept != 0, 1.0, 0.0)
    blocks = depth // BLOCK
    per_tile = LANES // blocks
    spread = jnp.where(iota((LANES, depth), 0) == iota((LANES, depth), 1) // BLOCK, 1.0, 0.0).astype(BF16)
    get_amps.wait()

    def mask_tile(tile, carry):
        block_rows = pattern[:, pl.ds(pl.multiple_of(tile * LANES, LANES), LANES)]
        turned = [
            block_rows if k == 0 else pltpu.roll(block_rows, LANES - k * blocks, 1) for k in range(per_tile)
        ]
        mask = jnp.dot(jnp.concatenate(turned, axis=0).astype(BF16), spread, preferred_element_type=F32)
        for k in range(per_tile):
            first_col = pl.multiple_of((tile * per_tile + k) * depth, LANES)
            values = amps[:, pl.ds(first_col, depth)].astype(F32)
            values = jnp.where(mask[k * rows : (k + 1) * rows] != 0.0, values, 0.0)
            outgoing[tile * per_tile + k] = fold(values).astype(BF16)
        return carry

    lax.fori_loop(0, n // per_tile, mask_tile, 0)
    incoming[core * chips + chip] = outgoing[me]

    pl.semaphore_wait(barrier, n - 1)

    def amps_copy(target, parity):
        return pltpu.make_async_remote_copy(
            src_ref=outgoing.at[target],
            dst_ref=incoming.at[core * chips + chip],
            send_sem=send_sem.at[parity],
            recv_sem=recv_sem.at[parity],
            device_id={"row": target},
            device_id_type=pl.DeviceIdType.MESH,
        )

    def send_unlike(k, carry):
        amps_copy(2 * lax.rem(chip + k, chips) + 1 - core, 0).start()
        return carry

    def send_like(k, carry):
        amps_copy(2 * lax.rem(chip + k, chips) + core, 1).start()
        return carry

    lax.fori_loop(0, chips, send_unlike, 0, unroll=unroll)
    lax.fori_loop(1, chips, send_like, 0, unroll=unroll)

    for copy in get_late:
        copy.wait()
    nvir = vir_irrep_ref.shape[0]
    highs = -(-nvir // LANES)
    high_rows = -(-highs // 8) * 8

    def table(ref):
        full = nvir // LANES
        pieces = [ref[i * LANES : (i + 1) * LANES].reshape(1, LANES).astype(F32) for i in range(full)]
        if nvir % LANES:
            rest = ref[full * LANES : nvir].reshape(1, nvir - full * LANES).astype(F32)
            pieces.append(jnp.concatenate([rest, jnp.zeros((1, LANES - nvir % LANES), F32)], axis=1))
        if high_rows > highs:
            pieces.append(jnp.zeros((high_rows - highs, LANES), F32))
        return jnp.concatenate(pieces, axis=0)

    energies = table(vir_energy_ref)
    top = energies.astype(BF16)
    rest = energies - top.astype(F32)
    middle = rest.astype(BF16)
    last = (rest - middle.astype(F32)).astype(BF16)
    tables = jnp.concatenate([table(vir_irrep_ref).astype(BF16), top, middle, last], axis=0)

    def batch_lookup(row):
        index = batch_pairs_ref[row : row + 1, :]
        low = jnp.bitwise_and(index, LANES - 1)
        high = lax.shift_right_logical(index, 7)
        onehot = jnp.where(iota((LANES, width), 0) == low, 1.0, 0.0).astype(BF16)
        found = jnp.dot(tables, onehot, preferred_element_type=F32)
        pick = iota((high_rows, width), 0) == high
        label = jnp.sum(jnp.where(pick, found[:high_rows], 0.0), axis=0, keepdims=True)
        energy = found[high_rows : 2 * high_rows] + found[2 * high_rows : 3 * high_rows] + found[3 * high_rows :]
        return label.astype(jnp.int32), jnp.sum(jnp.where(pick, energy, 0.0), axis=0, keepdims=True)

    label_a, energy_a = batch_lookup(0)
    label_b, energy_b = batch_lookup(1)
    batch_irrep = jnp.bitwise_xor(label_a, label_b)
    denom = (energy_a + energy_b) - occ_sum

    kept = jnp.zeros((blocks, width), jnp.int32)
    for label in range(IRREPS):
        kept = jnp.where(batch_irrep == label, upright(intp_ref[label : label + 1, :]), kept)
    kept = jnp.where(kept != 0, 1.0, 0.0)
    get_ints.wait()
    for b in range(blocks):
        keep = jnp.broadcast_to(kept[b : b + 1], (16, width)).astype(BF16)
        for i in range(BLOCK // 16):
            at = b * BLOCK + i * 16
            ints[at : at + 16, :] = ints[at : at + 16, :] * keep

    group = min(chips, 8)
    half = depth // 2

    def multiply(parity):
        def step(g, carry):
            planes = incoming[pl.ds(parity * chips + g * group, group)].astype(F32)
            left = planes[:, :rows].reshape(group * rows, half).astype(BF16)
            right = planes[:, rows:].reshape(group * rows, half).astype(BF16)
            product = jnp.dot(left, ints[:half, :], preferred_element_type=F32) + jnp.dot(
                right, ints[half:, :], preferred_element_type=F32
            )
            part[parity, pl.ds(g * group, group)] = product.reshape(group, rows, width)
            return carry

        lax.fori_loop(0, chips // group, step, 0)

    def wait_planes(sem, count):
        planes = incoming.at[pl.ds(0, count)]
        pltpu.make_async_copy(planes, planes, sem).wait()

    wait_planes(recv_sem.at[0], chips)
    multiply(1 - core)
    to_mate = pltpu.make_async_remote_copy(
        src_ref=part.at[1 - core],
        dst_ref=from_mate,
        send_sem=mate_sem.at[0],
        recv_sem=mate_sem.at[1],
        device_id={"row": mate},
        device_id_type=pl.DeviceIdType.MESH,
    )
    to_mate.start()
    wait_planes(recv_sem.at[1], chips - 1)
    multiply(core)
    to_mate.wait_recv()

    def wire_copy(target):
        return pltpu.make_async_remote_copy(
            src_ref=wire_out.at[target],
            dst_ref=wire_in.at[chip],
            send_sem=wire_sem.at[0],
            recv_sem=wire_sem.at[1],
            device_id={"row": 2 * target + core},
            device_id_type=pl.DeviceIdType.MESH,
        )

    def step_copy(target):
        return pltpu.make_async_remote_copy(
            src_ref=step_out.at[target],
            dst_ref=step_in.at[chip],
            send_sem=wire_sem.at[2],
            recv_sem=wire_sem.at[3],
            device_id={"row": 2 * target + core},
            device_id_type=pl.DeviceIdType.MESH,
        )

    def encode(g, carry):
        some = pl.ds(g * group, group)
        both = part[core, some] + from_mate[some]
        step = jnp.maximum(jnp.max(jnp.abs(both), axis=2, keepdims=True), TINY) * (1.0 / LEVELS)
        step_out[some] = flat(step)
        codes = jnp.round(both * (1.0 / step))
        codes = jnp.concatenate([codes[:, :, : width // 2], codes[:, :, width // 2 :]], axis=1)
        wire_out[some] = codes.astype(jnp.int32).astype(jnp.int16)
        return carry

    def send_sum(k, carry):
        target = lax.rem(chip + k, chips)
        step_copy(target).start()
        wire_copy(target).start()
        return carry

    lax.fori_loop(0, chips // group, encode, 0)
    lax.fori_loop(1, chips, send_sum, 0, unroll=unroll)
    step_in[chip] = step_out[chip]
    wire_in[chip] = wire_out[chip]

    arrived = wire_in.at[pl.ds(0, chips - 1)]
    steps_arrived = step_in.at[pl.ds(0, chips - 1)]
    pltpu.make_async_copy(steps_arrived, steps_arrived, wire_sem.at[3]).wait()
    pltpu.make_async_copy(arrived, arrived, wire_sem.at[1]).wait()

    def decode(g, total):
        some = pl.ds(g * group, group)
        step = tall(step_in[some], rows)
        codes = wire_in[some].astype(jnp.int32).astype(F32)
        left = jnp.sum(codes[:, :rows] * step, axis=0)
        right = jnp.sum(codes[:, rows:] * step, axis=0)
        return total + jnp.concatenate([left, right], axis=1)

    total = lax.fori_loop(0, chips // group, decode, const_ref[...])
    out_ref[...] = total / denom

    wait_planes(send_sem.at[0], chips)
    wait_planes(send_sem.at[1], chips - 1)
    to_mate.wait_send()
    sent = wire_out.at[pl.ds(0, chips - 1)]
    pltpu.make_async_copy(sent, sent, wire_sem.at[0]).wait()
    steps_sent = step_out.at[pl.ds(0, chips - 1)]
    pltpu.make_async_copy(steps_sent, steps_sent, wire_sem.at[2]).wait()


def per_device(
    n,
    amplitudes,
    integrals,
    constant,
    occ_pairs,
    batch_pairs,
    occ_irrep,
    vir_irrep,
    occ_energy,
    vir_energy,
    t2_pattern,
    int_pattern,
):
    rows = amplitudes.shape[0]
    depth, width = integrals.shape
    chips = n // 2
    vmem = pl.BlockSpec(memory_space=pltpu.VMEM)
    hbm = pl.BlockSpec(memory_space=pl.ANY)
    return pl.pallas_call(
        functools.partial(kernel, n),
        out_shape=jax.ShapeDtypeStruct((rows, width), F32),
        in_specs=[hbm] * 11,
        out_specs=vmem,
        scratch_shapes=[
            pltpu.VMEM((rows, n * depth), BF16),
            pltpu.VMEM((depth, width), BF16),
            pltpu.VMEM(constant.shape, F32),
            pltpu.VMEM(occ_pairs.shape[::-1], jnp.int32),
            pltpu.VMEM(batch_pairs.shape[::-1], jnp.int32),
            pltpu.VMEM(occ_irrep.shape, jnp.int32),
            pltpu.VMEM(vir_irrep.shape, jnp.int32),
            pltpu.VMEM(occ_energy.shape, F32),
            pltpu.VMEM(vir_energy.shape, F32),
            pltpu.VMEM(t2_pattern.shape, jnp.int32),
            pltpu.VMEM(int_pattern.shape[::-1], jnp.int32),
            pltpu.VMEM((rows, t2_pattern.shape[1]), F32),
            pltpu.VMEM((n, 2 * rows, depth // 2), BF16),
            pltpu.VMEM((n, 2 * rows, depth // 2), BF16),
            pltpu.VMEM((2, chips, rows, width), F32),
            pltpu.VMEM((chips, rows, width), F32),
            pltpu.VMEM((chips, 2 * rows, width // 2), jnp.int16),
            pltpu.VMEM((chips, 2 * rows, width // 2), jnp.int16),
            pltpu.VMEM((chips, 1, LANES), F32),
            pltpu.VMEM((chips, 1, LANES), F32),
            pltpu.SemaphoreType.DMA((11,)),
            pltpu.SemaphoreType.DMA((2,)),
            pltpu.SemaphoreType.DMA((2,)),
            pltpu.SemaphoreType.DMA((2,)),
            pltpu.SemaphoreType.DMA((4,)),
        ],
        compiler_params=pltpu.CompilerParams(
            collective_id=0, has_side_effects=True, vmem_limit_bytes=60 * 1024 * 1024
        ),
        cost_estimate=pl.CostEstimate(
            flops=2 * n * rows * depth * width, bytes_accessed=2 * depth * width, transcendentals=0
        ),
    )(
        amplitudes,
        integrals,
        constant,
        occ_pairs.T,
        batch_pairs.T,
        occ_irrep,
        vir_irrep,
        occ_energy,
        vir_energy,
        t2_pattern,
        int_pattern.T,
    )


def solution(mesh):
    in_specs = (
        P(("groups", "row"), None),
        P("row", "groups"),
        P("row", "groups"),
        P(("groups", "row"), None),
        P("groups", None),
        P("groups"),
        P("groups"),
        P("groups"),
        P("groups"),
        P(None, "groups"),
        P(("groups", "row"), None),
    )
    out_specs = P("row", "groups")
    return jax.shard_map(
        functools.partial(per_device, mesh.shape["row"]),
        mesh=mesh,
        in_specs=in_specs,
        out_specs=out_specs,
        check_vma=False,
    )
```
